256 devices in a mesh: grp: 16 (over y, x), sp: 8 (over z), tp: 2 (over core).
Axes of the slice: x: 4, y: 4, z: 8, core: 2. Of those that a mesh axis runs over, the one named last changes fastest.
Arguments:
- q_spatial: bfloat16 [32768, 3072], P(('grp', 'sp'), 'tp'), may hold values from -130 to 130
- k_spatial: bfloat16 [32768, 3072], P(('grp', 'sp'), 'tp'), may hold values from -5 to 5
- v_spatial: bfloat16 [32768, 3072], P(('grp', 'sp'), 'tp'), may hold values from -6 to 6
- q_temporal: bfloat16 [32768, 3072], P(('grp', 'sp'), 'tp'), may hold values from -130 to 130
- k_temporal: bfloat16 [32768, 3072], P(('grp', 'sp'), 'tp'), may hold values from -5 to 5
- out_weight: bfloat16 [3072, 3072], P('tp', ('grp', 'sp')), may hold values from -0.109375 to 0.109375
- frame_video: int32 [256], replicated, may hold values from 0 to 15, never falling along the last dimension, each value on 1 to 32 neighbouring positions
- video_patches: int32 [16], replicated, may hold values from 64 to 128, as said below
Outputs:
- mixed: bfloat16 [32768, 3072], P(('grp', 'sp'), 'tp')
The draws below stay inside these ranges and needn't reach their ends.
Inputs may be any that keep to these rules, and one draw needn't show every extreme that they name: `video_patches`: between 64 and 128; some video has exactly 128.
All inputs are finite; a program needn't handle non-finite values.
Results may differ from the reference program's by a relative error of at most 0.014.
Values may be sent and summed in bfloat16 or wider, within the bound.
A program may use at most 128 MiB of HBM per device.

```python
import math
import jax
import jax.numpy as jnp
import numpy as np
from jax import lax

HEADS = 24
HD = 128
D = 3072
PMAX = 128
HF = 3072
NF = 256
VIDEOS = 16
FMAX = 32


def shared_keys(key, salt):
    base = jax.random.normal(jax.random.fold_in(key, salt), (NF * PMAX, HEADS * HD), jnp.float32)
    return jnp.clip(base, -5.0, 5.0)


def drawn_queries(key, shared):
    own = jax.random.normal(key, shared.shape, jnp.float32)
    return jnp.clip(own, -6.0, 6.0)


def draw_q_spatial(key, part):
    shared = shared_keys(key, 77)
    key = jax.random.fold_in(key, 11)
    return drawn_queries(key, shared).astype(jnp.bfloat16)


def draw_k_spatial(key, part):
    shared = shared_keys(key, 77)
    return shared.astype(jnp.bfloat16)


def draw_q_temporal(key, part):
    shared = shared_keys(key, 78)
    key = jax.random.fold_in(key, 13)
    return drawn_queries(key, shared).astype(jnp.bfloat16)


def draw_k_temporal(key, part):
    shared = shared_keys(key, 78)
    return shared.astype(jnp.bfloat16)


def draw_video_patches(key, part):
    key = jax.random.fold_in(key, 15)
    values = jax.random.randint(key, (VIDEOS,), PMAX // 2, PMAX + 1)
    widest = jax.random.randint(jax.random.fold_in(key, 4), (), 0, VIDEOS)
    values = jnp.where(jnp.arange(VIDEOS) == widest, PMAX, values)
    return values.astype(jnp.int32)


def block_scale(key, extent, pieces, least, largest):
    def one(dim, blocks):
        heights = jax.random.uniform(jax.random.fold_in(jax.random.fold_in(key, 6), dim), (blocks,), jnp.float32, least / len(pieces), largest / len(pieces))
        return jnp.repeat(jnp.exp(heights), extent[dim] // blocks).reshape((-1,) + (1,) * (len(extent) - dim - 1))

    factor_of = one(*pieces[0])
    for cut in pieces[1:]:
        factor_of = factor_of * one(*cut)
    return factor_of


def length_profile(amount, total, bound, slope):
    weights = [(1 << 20) // math.isqrt(standing ** slope) + 1 for standing in range(2, amount + 1)]
    surplus, counts = total - bound - (amount - 1), [1] * (amount - 1)
    while surplus > 0:
        candidates = [i for i in range(amount - 1) if counts[i] < bound]
        pool, remaining = sum([weights[i] for i in candidates]), surplus
        for i in candidates:
            extra = min(bound - counts[i], max(1, remaining * weights[i] // pool), surplus)
            counts[i] = counts[i] + extra
            surplus = surplus - extra
    return np.array([bound] + counts)


def uneven(own_key, amount, total, reach, lean):
    if amount == 2:
        one = jax.random.randint(own_key, (), max(1, total - reach), min(reach, total - 1) + 1)
        return jnp.stack([one, total - one])
    sizes = jnp.asarray(length_profile(amount, total, reach, lean), jnp.int32)
    couples = (amount - 1) // 2
    giver, taker = sizes[1:1 + 2 * couples:2], sizes[2:2 + 2 * couples:2]
    room = jnp.minimum(giver - 1, reach - taker)
    moved = jax.random.randint(jax.random.fold_in(own_key, 1), (couples,), 0, 1 << 20) % (room + 1)
    sizes = sizes.at[1:1 + 2 * couples:2].set(giver - moved).at[2:2 + 2 * couples:2].set(taker + moved)
    return sizes[jax.random.permutation(jax.random.fold_in(own_key, 2), amount)]


def normal_values(own_key, dims, deviation, bound, shards=(), held_as=jnp.bfloat16):
    entries = jax.random.normal(own_key, dims, jnp.float32) * deviation
    if len(shards) > 0:
        entries = block_scale(own_key, dims, shards, -0.22, 0.18) * entries
    return jnp.clip(entries, min=-bound, max=bound).astype(held_as)


def setup_inputs(seed: int = 0) -> dict:
    seeds = jax.random.split(jax.random.key(seed), 9)
    return {
        "q_spatial": draw_q_spatial(jax.random.fold_in(seeds[8], 71), 0),
        "k_spatial": draw_k_spatial(jax.random.fold_in(seeds[8], 71), 0),
        "v_spatial": normal_values(seeds[2], (NF * PMAX, HF), 1.0, 6.0, ((0, 128), (1, 2))),
        "q_temporal": draw_q_temporal(jax.random.fold_in(seeds[8], 71), 0),
        "k_temporal": draw_k_temporal(jax.random.fold_in(seeds[8], 71), 0),
        "out_weight": normal_values(seeds[5], (HF, D), HF ** -0.5, 0.109375, ((0, 2), (1, 128))),
        "frame_video": jnp.searchsorted(jnp.cumsum(uneven(seeds[6], VIDEOS, NF, FMAX, 0)), jnp.arange(NF), side="right").astype(jnp.int32),
        "video_patches": draw_video_patches(jax.random.fold_in(seeds[8], 71), 0),
    }


def soft_weights(scores, mask):
    masked = jnp.where(mask, scores, jnp.float32(-1e30))
    top = jnp.max(masked, axis=-1, keepdims=True)
    expo = jnp.where(mask, jnp.exp(scores - top), jnp.float32(0.0))
    return (expo / jnp.sum(expo, axis=-1, keepdims=True)).astype(jnp.bfloat16)


def reference(q_spatial, k_spatial, v_spatial, q_temporal, k_temporal, out_weight, frame_video, video_patches):
    scale = HD ** -0.5
    frame_patches = video_patches[frame_video]
    live = jnp.arange(PMAX, dtype=jnp.int32)[None, :] < frame_patches[:, None]
    shape4 = (NF, PMAX, HEADS, HD)

    def spatial_frame(items):
        query, key_rows, values, alive = items
        scores = jnp.einsum("phd,khd->hpk", query.astype(jnp.float32), key_rows.astype(jnp.float32)) * scale
        weights = soft_weights(scores, alive[None, None, :])
        result = jnp.einsum("hpk,khd->phd", weights.astype(jnp.float32), values.astype(jnp.float32))
        return result.astype(jnp.bfloat16)

    spatial = lax.map(spatial_frame, (q_spatial.reshape(shape4), k_spatial.reshape(shape4), v_spatial.reshape(shape4), live))
    same = frame_video[:, None] == frame_video[None, :]

    def temporal_patch(items):
        query, key_rows, values = items
        scores = jnp.einsum("fhd,ghd->hfg", query.astype(jnp.float32), key_rows.astype(jnp.float32)) * scale
        weights = soft_weights(scores, same[None, :, :])
        result = jnp.einsum("hfg,ghd->fhd", weights.astype(jnp.float32), values.astype(jnp.float32))
        return result.astype(jnp.bfloat16)

    by_patch = (jnp.transpose(q_temporal.reshape(shape4), (1, 0, 2, 3)), jnp.transpose(k_temporal.reshape(shape4), (1, 0, 2, 3)), jnp.transpose(spatial, (1, 0, 2, 3)))
    temporal = jnp.transpose(lax.map(temporal_patch, by_patch), (1, 0, 2, 3)).reshape(NF, PMAX, HEADS * HD)

    def project(items):
        rows_in, alive = items
        product = jnp.dot(rows_in, out_weight, preferred_element_type=jnp.float32)
        return jnp.where(alive[:, None], product, jnp.float32(0.0)).astype(jnp.bfloat16)

    mixed = lax.map(project, (temporal, live))
    return mixed.reshape(NF * PMAX, D)
```

```python
import functools

import jax
import jax.numpy as jnp
from jax import lax
from jax.experimental import pallas as pl
from jax.experimental.pallas import tpu as pltpu
from jax.sharding import PartitionSpec as P

MESH = pl.DeviceIdType.MESH
HD = 128
PMAX = 128
NY, NX, NZ = 4, 4, 8
GROUPS = NY * NX * NZ
F32 = jnp.float32
BF16 = jnp.bfloat16
NT = (((1,), (1,)), ((), ()))
NN = (((1,), (0,)), ((), ()))


def softmax_rows(scores, mask):
    masked = jnp.where(mask, scores, F32(-1e30))
    top = jnp.max(masked, axis=-1, keepdims=True)
    expo = jnp.exp(masked - top)
    return (expo / jnp.sum(expo, axis=-1, keepdims=True)).astype(BF16)


def kernel(
    heads,
    qs, ks, vs, qt, kt, w, fv_col, fv_row, patches,
    out,
    stage, qk_send, qk_recv, v_send, v_recv, o_send, o_recv, weights, mixed_in, wa, wb, wfull, part, part_recv, own,
    sem_qk, sem_v, sem_o, sem_part_s, sem_part_r, sem_wz_s, sem_wz_r, sem_w1_s, sem_w1_r, sem_w2_s, sem_w2_r,
):
    grp = lax.axis_index("grp")
    z = lax.axis_index("sp")
    core = lax.axis_index("tp")
    y, x = grp // NX, grp % NX
    me = grp * NZ + z
    rows = 2 * heads
    cols = w.shape[1]
    half = heads * HD // 2

    def peer(i):
        dy, dx, dz = i // (NX * NZ), (i // NZ) % NX, i % NZ
        g2 = ((y + dy) % NY) * NX + (x + dx) % NX
        return g2, (z + dz) % NZ

    def at_x(d):
        return {"grp": y * NX + (x + d + NX) % NX}

    def at_y(d):
        return {"grp": ((y + d + NY) % NY) * NX + x}

    def at_z(d):
        return {"sp": (z + d + NZ) % NZ}

    barrier = pltpu.get_barrier_semaphore()

    def greet(i, carry):
        g2, s2 = peer(i)
        pl.semaphore_signal(barrier, inc=1, device_id={"grp": g2, "sp": s2}, device_id_type=MESH)
        return carry

    lax.fori_loop(1, GROUPS, greet, 0)
    pl.semaphore_signal(barrier, inc=1, device_id={"tp": 1 - core}, device_id_type=MESH)

    eye = (
        lax.broadcasted_iota(jnp.int32, (cols, cols), 0) == lax.broadcasted_iota(jnp.int32, (cols, cols), 1)
    ).astype(BF16)
    turned = lax.dot_general(eye, w[...], NT, preferred_element_type=F32).astype(BF16)
    wa[x, y, z] = turned[:, :half]
    wb[y, x, z] = turned[:, half:]

    def to_stage(value, frame, head, base, height):
        stage[pl.ds(base + frame * heads + head, PMAX, stride=height), :] = value.astype(F32)

    def to_chunks(dst, height):
        def body(i, carry):
            block = stage[pl.ds(pl.multiple_of(i * 16 * height, 16), 16 * height), :]
            dst[pl.ds(i * 16, 16)] = block.reshape(16, height, HD).astype(BF16)
            return carry

        lax.fori_loop(0, GROUPS // 16, body, 0)

    def from_chunks(src, height):
        def body(i, carry):
            block = src[pl.ds(i * 16, 16)].astype(F32)
            stage[pl.ds(pl.multiple_of(i * 16 * height, 16), 16 * height), :] = block.reshape(16 * height, HD)
            return carry

        lax.fori_loop(0, GROUPS // 16, body, 0)

    def head_rows(frame, head, base, height):
        return stage[pl.ds(base + frame * heads + head, PMAX, stride=height), :]

    for n, src in enumerate((qt, kt)):
        for f in range(2):
            for h in range(heads):
                to_stage(src[f * PMAX : (f + 1) * PMAX, h * HD : (h + 1) * HD], f, h, n * rows, 2 * rows)
    to_chunks(qk_send, 2 * rows)

    pl.semaphore_wait(barrier, GROUPS)

    def w_copy(src, dst, send, recv, where):
        return pltpu.make_async_remote_copy(
            src_ref=src, dst_ref=dst, send_sem=send, recv_sem=recv, device_id=where, device_id_type=MESH
        )

    def z_copies(step, sign):
        zz = (z - sign * step + NZ) % NZ
        lane = 0 if sign > 0 else 1
        spot = [lane, step]
        return [
            w_copy(wa.at[x, y, zz], wa.at[x, y, zz], sem_wz_s.at[0, lane, step], sem_wz_r.at[0, lane, step], at_z(sign)),
            w_copy(wb.at[y, x, zz], wb.at[y, x, zz], sem_wz_s.at[1, lane, step], sem_wz_r.at[1, lane, step], at_z(sign)),
        ]

    z_plan = [(0, 1), (0, -1), (1, 1), (1, -1), (2, 1), (2, -1), (3, 1)]
    for step, sign in z_plan[:2]:
        for c in z_copies(step, sign):
            c.start()

    def exchange(send_buf, recv_buf, sems):
        def copy(i):
            g2, s2 = peer(i)
            return pltpu.make_async_remote_copy(
                src_ref=send_buf.at[g2 * NZ + s2], dst_ref=recv_buf.at[me], send_sem=sems.at[0], recv_sem=sems.at[1],
                device_id={"grp": g2, "sp": s2}, device_id_type=MESH,
            )

        def body(i, carry):
            copy(i).start()
            return carry

        lax.fori_loop(1, GROUPS, body, 0)
        recv_buf[me] = send_buf[me]

        return pltpu.make_async_remote_copy(
            src_ref=send_buf.at[pl.ds(0, GROUPS - 1)], dst_ref=recv_buf.at[pl.ds(0, GROUPS - 1)],
            send_sem=sems.at[0], recv_sem=sems.at[1], device_id={"tp": core}, device_id_type=MESH,
        )

    sent_qk = exchange(qk_send, qk_recv, sem_qk)

    scale = F32(HD**-0.5)
    key_at = lax.broadcasted_iota(jnp.int32, (PMAX, PMAX), 1)

    for f in range(2):
        for h in range(heads):
            at = (slice(f * PMAX, (f + 1) * PMAX), slice(h * HD, (h + 1) * HD))
            scores = lax.dot_general(qs[at], ks[at], NT, preferred_element_type=F32) * scale
            probs = softmax_rows(scores, key_at < patches[f])
            value = lax.dot_general(probs, vs[at], NN, preferred_element_type=F32)
            to_stage(value.astype(BF16), f, h, 0, rows)
    to_chunks(v_send, rows)
    sent_v = exchange(v_send, v_recv, sem_v)

    for n, (step, sign) in enumerate(z_plan):
        for c in z_copies(step, sign):
            c.wait_recv()
        if n + 2 < len(z_plan):
            for c in z_copies(*z_plan[n + 2]):
                c.start()

    def first_copies(sign):
        lane = 0 if sign > 0 else 1
        return [
            w_copy(wa.at[x, y], wa.at[x, y], sem_w1_s.at[0, lane], sem_w1_r.at[0, lane], at_y(sign)),
            w_copy(wb.at[y, x], wb.at[y, x], sem_w1_s.at[1, lane], sem_w1_r.at[1, lane], at_x(sign)),
        ]

    def first_forward(sign):
        lane = 2 if sign > 0 else 3
        part_z = pl.ds(0, NZ // 2) if sign > 0 else pl.ds(NZ // 2, NZ // 2)
        yy, xx = (y - sign + NY) % NY, (x - sign + NX) % NX
        return [
            w_copy(wa.at[x, yy, part_z], wa.at[x, yy, part_z], sem_w1_s.at[0, lane], sem_w1_r.at[0, lane], at_y(sign)),
            w_copy(wb.at[y, xx, part_z], wb.at[y, xx, part_z], sem_w1_s.at[1, lane], sem_w1_r.at[1, lane], at_x(sign)),
        ]

    for sign in (1, -1):
        for c in first_copies(sign):
            c.start()
    for sign in (1, -1):
        for c in first_copies(sign):
            c.wait_recv()
        for c in first_forward(sign):
            c.start()

    def second_copies(sign, j):
        lane = 0 if sign > 0 else 1
        return [
            w_copy(wa.at[x, j], wa.at[x, j], sem_w2_s.at[0, lane, j], sem_w2_r.at[0, lane, j], at_x(sign)),
            w_copy(wb.at[y, j], wb.at[y, j], sem_w2_s.at[1, lane, j], sem_w2_r.at[1, lane, j], at_y(sign)),
        ]

    def second_forward(sign, j):
        lane = 2 if sign > 0 else 3
        yy, xx = (y - sign + NY) % NY, (x - sign + NX) % NX
        return [
            w_copy(wa.at[xx, j], wa.at[xx, j], sem_w2_s.at[0, lane, j], sem_w2_r.at[0, lane, j], at_x(sign)),
            w_copy(wb.at[yy, j], wb.at[yy, j], sem_w2_s.at[1, lane, j], sem_w2_r.at[1, lane, j], at_y(sign)),
        ]

    for sign in (1, -1):
        for c in first_forward(sign):
            c.wait_recv()
    for j in range(4):
        for sign in (1, -1):
            for c in second_copies(sign, j):
                c.start()

    sent_qk.wait_recv()
    from_chunks(qk_recv, 2 * rows)
    same = fv_col[...] == fv_row[...]
    for h in range(heads):
        q = jnp.concatenate([head_rows(f, h, 0, 2 * rows) for f in range(2)], axis=0).astype(BF16)
        k = jnp.concatenate([head_rows(f, h, rows, 2 * rows) for f in range(2)], axis=0).astype(BF16)
        scores = lax.dot_general(q, k, NT, preferred_element_type=F32) * scale
        weights[h] = softmax_rows(scores, same)

    for j in range(4):
        for sign in (1, -1):
            for c in second_copies(sign, j):
                c.wait_recv()
            if (j < 2) == (sign > 0):
                for c in second_forward(sign, j):
                    c.start()

    sent_v.wait_recv()
    from_chunks(v_recv, rows)
    for h in range(heads):
        v = jnp.concatenate([head_rows(f, h, 0, rows) for f in range(2)], axis=0).astype(BF16)
        value = lax.dot_general(weights[h], v, NN, preferred_element_type=F32)
        mixed_in[:, h * HD : (h + 1) * HD] = value.astype(BF16)

    for sign in (1, -1):
        for j in range(4):
            if (j < 2) == (sign > 0):
                for c in second_forward(sign, j):
                    c.wait_recv()

    def repack(i, carry):
        yy, xx = i // NX, i % NX
        at = pl.ds(pl.multiple_of(i * NZ * cols, 16), NZ * cols)
        wfull[at, :half] = wa[xx, yy].astype(F32).reshape(NZ * cols, half).astype(BF16)
        wfull[at, half:] = wb[yy, xx].astype(F32).reshape(NZ * cols, half).astype(BF16)
        return carry

    lax.fori_loop(0, NY * NX, repack, 0)

    blocks, _, width = part.shape
    mine = blocks * width

    def product(first, i):
        at = pl.ds(pl.multiple_of(first * mine + i * width, 16), width)
        return lax.dot_general(mixed_in[...], wfull[at, :], NT, preferred_element_type=F32)

    def part_copy(i):
        return pltpu.make_async_remote_copy(
            src_ref=part.at[i], dst_ref=part_recv.at[i], send_sem=sem_part_s.at[i], recv_sem=sem_part_r.at[i],
            device_id={"tp": 1 - core}, device_id_type=MESH,
        )

    def give(i, carry):
        part[i] = product(1 - core, i)
        part_copy(i).start()
        return carry

    lax.fori_loop(0, blocks, give, 0)

    def keep(i, carry):
        own[i] = product(core, i)
        return carry

    lax.fori_loop(0, blocks, keep, 0)
    for i in range(blocks):
        part_copy(i).wait_recv()
        total = own[i] + part_recv[i]
        for f in range(2):
            for j in range(width // HD):
                to_stage(total[f * PMAX : (f + 1) * PMAX, j * HD : (j + 1) * HD], f, i * (width // HD) + j, 0, rows)
    to_chunks(o_send, rows)
    sent_o = exchange(o_send, o_recv, sem_o)

    sent_qk.wait_send()
    sent_v.wait_send()
    for i in range(blocks):
        part_copy(i).wait_send()
    for step, sign in z_plan:
        for c in z_copies(step, sign):
            c.wait_send()
    for sign in (1, -1):
        for c in first_copies(sign) + first_forward(sign):
            c.wait_send()
        for j in range(4):
            for c in second_copies(sign, j):
                c.wait_send()
            if (j < 2) == (sign > 0):
                for c in second_forward(sign, j):
                    c.wait_send()

    sent_o.wait_recv()
    from_chunks(o_recv, rows)
    row_at = lax.broadcasted_iota(jnp.int32, (PMAX, HD), 0)
    for f in range(2):
        alive = row_at < patches[f]
        for h in range(heads):
            value = jnp.where(alive, head_rows(f, h, 0, rows), F32(0.0))
            out[f * PMAX : (f + 1) * PMAX, h * HD : (h + 1) * HD] = value.astype(BF16)
    sent_o.wait_send()


def per_device(q_spatial, k_spatial, v_spatial, q_temporal, k_temporal, out_weight, frame_video, video_patches):
    rows, feats = q_spatial.shape
    heads = feats // HD
    cols = out_weight.shape[1]
    frames = rows // PMAX
    first = lax.axis_index(("grp", "sp")) * frames
    my_video = lax.dynamic_slice_in_dim(frame_video, first, frames)
    match = my_video[:, None] == jnp.arange(video_patches.shape[0], dtype=jnp.int32)[None, :]
    patches = jnp.sum(jnp.where(match, video_patches[None, :], 0), axis=1).astype(jnp.int32)
    by_slot = frame_video.reshape(GROUPS, frames).T.reshape(-1)
    vmem = pl.BlockSpec(memory_space=pltpu.VMEM)
    chunk = frames * heads
    blocks = 4
    width = feats // blocks
    all_frames = frame_video.shape[0]
    dma = pltpu.SemaphoreType.DMA
    return pl.pallas_call(
        functools.partial(kernel, heads),
        out_shape=jax.ShapeDtypeStruct((rows, feats), BF16),
        in_specs=[vmem] * 8 + [pl.BlockSpec(memory_space=pltpu.SMEM)],
        out_specs=vmem,
        scratch_shapes=[
            pltpu.VMEM((GROUPS * 2 * chunk, HD), F32),
            pltpu.VMEM((GROUPS, 2 * chunk, HD), BF16),
            pltpu.VMEM((GROUPS, 2 * chunk, HD), BF16),
            pltpu.VMEM((GROUPS, chunk, HD), BF16),
            pltpu.VMEM((GROUPS, chunk, HD), BF16),
            pltpu.VMEM((GROUPS, chunk, HD), BF16),
            pltpu.VMEM((GROUPS, chunk, HD), BF16),
            pltpu.VMEM((heads, all_frames, all_frames), BF16),
            pltpu.VMEM((all_frames, feats), BF16),
            pltpu.VMEM((NX, NY, NZ, cols, feats // 2), BF16),
            pltpu.VMEM((NY, NX, NZ, cols, feats // 2), BF16),
            pltpu.VMEM((GROUPS * cols, feats), BF16),
            pltpu.VMEM((blocks, all_frames, width), F32),
            pltpu.VMEM((blocks, all_frames, width), F32),
            pltpu.VMEM((blocks, all_frames, width), F32),
            dma((2,)),
            dma((2,)),
            dma((2,)),
            dma((blocks,)),
            dma((blocks,)),
            dma((2, 2, 4)),
            dma((2, 2, 4)),
            dma((2, 4)),
            dma((2, 4)),
            dma((2, 4, 4)),
            dma((2, 4, 4)),
        ],
        compiler_params=pltpu.CompilerParams(
            collective_id=0, has_side_effects=True, vmem_limit_bytes=58 * 2**20
        ),
    )(
        q_spatial, k_spatial, v_spatial, q_temporal, k_temporal, out_weight,
        by_slot[:, None], by_slot[None, :], patches,
    )


def solution(mesh):
    return jax.shard_map(
        per_device,
        mesh=mesh,
        in_specs=(
            P(("grp", "sp"), "tp"),
            P(("grp", "sp"), "tp"),
            P(("grp", "sp"), "tp"),
            P(("grp", "sp"), "tp"),
            P(("grp", "sp"), "tp"),
            P("tp", ("grp", "sp")),
            P(),
            P(),
        ),
        out_specs=P(("grp", "sp"), "tp"),
        check_vma=False,
    )
```

```python
import functools

import jax
import jax.numpy as jnp
from jax import lax
from jax.experimental import pallas as pl
from jax.experimental.pallas import tpu as pltpu
from jax.sharding import PartitionSpec as P

MESH = pl.DeviceIdType.MESH
HD = 128
PMAX = 128
NY, NX, NZ = 4, 4, 8
GROUPS = NY * NX * NZ
PARTS = 3
F32 = jnp.float32
BF16 = jnp.bfloat16
NT = (((1,), (1,)), ((), ()))
NN = (((1,), (0,)), ((), ()))


def softmax_rows(scores, mask):
    masked = jnp.where(mask, scores, F32(-1e30))
    top = jnp.max(masked, axis=-1, keepdims=True)
    expo = jnp.exp(masked - top)
    return (expo / jnp.sum(expo, axis=-1, keepdims=True)).astype(BF16)


def kernel(
    heads, parts,
    qs, ks, vs, qt, kt, w, fv_col, fv_row, patches,
    out,
    stage, f_send, f_recv, o_send, o_recv, tall, wy, wfull, part, part_recv, own,
    sem_f, sem_o, sem_t_s, sem_t_r, sem_part_s, sem_part_r, sem_wz_s, sem_wz_r, sem_wy_s, sem_wy_r,
):
    grp = lax.axis_index("grp")
    z = lax.axis_index("sp")
    core = lax.axis_index("tp")
    y, x = grp // NX, grp % NX
    me = grp * NZ + z
    cols = w.shape[1]
    per = heads // parts
    height = f_send.shape[2]

    def peer(i):
        dy, dx, dz = i // (NX * NZ), (i // NZ) % NX, i % NZ
        g2 = ((y + dy) % NY) * NX + (x + dx) % NX
        return g2, (z + dz) % NZ

    barrier = pltpu.get_barrier_semaphore()

    def greet(i, carry):
        g2, s2 = peer(i)
        pl.semaphore_signal(barrier, inc=1, device_id={"grp": g2, "sp": s2}, device_id_type=MESH)
        return carry

    lax.fori_loop(1, GROUPS, greet, 0)
    pl.semaphore_signal(barrier, inc=1, device_id={"tp": 1 - core}, device_id_type=MESH)

    def remote(src, dst, send, recv, where):
        return pltpu.make_async_remote_copy(
            src_ref=src, dst_ref=dst, send_sem=send, recv_sem=recv, device_id=where, device_id_type=MESH
        )

    eye = (
        lax.broadcasted_iota(jnp.int32, (cols, cols), 0) == lax.broadcasted_iota(jnp.int32, (cols, cols), 1)
    ).astype(BF16)
    wy[y, z] = lax.dot_general(eye, w[...], NT, preferred_element_type=F32).astype(BF16)

    scale = F32(HD**-0.5)
    key_at = lax.broadcasted_iota(jnp.int32, (PMAX, PMAX), 1)

    def build(n):
        for f in range(2):
            rows = slice(f * PMAX, (f + 1) * PMAX)
            for j in range(per):
                at = (rows, slice((n * per + j) * HD, (n * per + j + 1) * HD))
                scores = lax.dot_general(qs[at], ks[at], NT, preferred_element_type=F32) * scale
                probs = softmax_rows(scores, key_at < patches[f])
                value = lax.dot_general(probs, vs[at], NN, preferred_element_type=F32)
                spot = f * per + j
                stage[pl.ds(spot, PMAX, stride=height), :] = qt[at].astype(F32)
                stage[pl.ds(2 * per + spot, PMAX, stride=height), :] = kt[at].astype(F32)
                stage[pl.ds(4 * per + spot, PMAX, stride=height), :] = value

        def pack(i, carry):
            block = stage[pl.ds(pl.multiple_of(i * 16 * height, 16), 16 * height), :]
            f_send[n, pl.ds(i * 16, 16)] = block.reshape(16, height, HD).astype(BF16)
            return carry

        lax.fori_loop(0, GROUPS // 16, pack, 0)

    def unpack(src):
        def body(i, carry):
            block = src[pl.ds(i * 16, 16)].astype(F32)
            stage[pl.ds(pl.multiple_of(i * 16 * height, 16), 16 * height), :] = block.reshape(16 * height, HD)
            return carry

        lax.fori_loop(0, GROUPS // 16, body, 0)

    def exchange(send_buf, recv_buf, sems, first, last):
        def body(i, carry):
            g2, s2 = peer(i)
            remote(send_buf.at[g2 * NZ + s2], recv_buf.at[me], sems.at[0], sems.at[1], {"grp": g2, "sp": s2}).start()
            return carry

        lax.fori_loop(first, last, body, 0)

    def exchanged(send_buf, recv_buf, sems):
        rest = pl.ds(0, GROUPS - 1)
        return remote(send_buf.at[rest], recv_buf.at[rest], sems.at[0], sems.at[1], {"tp": core})

    def z_copy(d):
        return remote(wy.at[y, z], wy.at[y, z], sem_wz_s.at[d], sem_wz_r.at[d], {"sp": (z + d) % NZ})

    def y_copy(e, d):
        zz = (z - e + NZ) % NZ
        return remote(
            wy.at[y, zz], wy.at[y, zz], sem_wy_s.at[e, d - 1], sem_wy_r.at[e, d - 1],
            {"grp": ((y + d) % NY) * NX + x},
        )

    def t_copy(n, k, d):
        at = (y + k) % NY
        return remote(
            tall.at[n, x, at], tall.at[n, x, at], sem_t_s.at[n, k, d - 1], sem_t_r.at[n, k, d - 1],
            {"grp": y * NX + (x + d) % NX},
        )

    z_order = (0, 1, 7, 2, 6, 3, 5, 4)
    around = (1, 3, 2)
    plane = NX * NZ

    build(0)
    pl.semaphore_wait(barrier, GROUPS)
    for e in (4, 3, 5, 2, 6, 1, 7):
        z_copy(e).start()
    exchange(f_send.at[0], f_recv.at[0], sem_f.at[0], 1, GROUPS)
    build(1)
    for n, e in enumerate(z_order):
        if e > 0:
            z_copy(e).wait_recv()
        for d in around:
            y_copy(e, d).start()
        first = n * (GROUPS // NZ)
        exchange(f_send.at[1], f_recv.at[1], sem_f.at[1], max(first, 1), first + GROUPS // NZ)
    build(2)
    exchange(f_send.at[2], f_recv.at[2], sem_f.at[2], 1, GROUPS)
    for n in range(parts):
        f_recv[n, me] = f_send[n, me]

    odd = x % 2
    third = NZ * cols
    small = third // 3

    def order_weights():
        for e in z_order:
            for d in around:
                y_copy(e, d).wait_recv()
        for yy in range(NY):
            block = wy[yy].astype(F32).reshape(third, heads * HD)
            base = (yy // 2) * 2 * third
            big = jnp.where(odd == 0, block[: 2 * small], block[small:]).astype(BF16)
            wfull[base + (yy % 2) * 2 * small : base + (yy % 2 + 1) * 2 * small, :] = big
            rest = jnp.where(odd == 0, block[2 * small :], block[:small]).astype(BF16)
            spot = odd + (yy % 2) - 2 * odd * (yy % 2)
            wfull[pl.ds(pl.multiple_of(base + 4 * small + spot * small, 16), small), :] = rest

    same = fv_col[...] == fv_row[...]
    for n in range(parts):
        if n == parts - 1:
            order_weights()
        exchanged(f_send.at[n], f_recv.at[n], sem_f.at[n]).wait_recv()
        unpack(f_recv.at[n])
        for j in range(per):
            q, k, v = (
                jnp.concatenate(
                    [stage[pl.ds(t * 2 * per + f * per + j, GROUPS, stride=height), :] for f in range(2)], axis=0
                ).astype(BF16)
                for t in range(3)
            )
            scores = lax.dot_general(q, k, NT, preferred_element_type=F32) * scale
            probs = softmax_rows(scores, same)
            value = lax.dot_general(probs, v, NN, preferred_element_type=F32)
            for k in range(NY):
                for f in range(2):
                    rows = value[f * GROUPS + k * plane : f * GROUPS + (k + 1) * plane]
                    tall[n, x, k, f * plane : (f + 1) * plane, j * HD : (j + 1) * HD] = rows.astype(BF16)
        for k in range(NY):
            for d in around:
                t_copy(n, k, d).start()

    width = 2 * third
    feats = per * HD

    def product(k, c):
        total = None
        for n in range(parts):
            left = jnp.concatenate([tall[n, s, (y + k) % NY] for s in range(NX)], axis=0)
            right = wfull[pl.ds(pl.multiple_of(c * width, 16), width), n * feats : (n + 1) * feats]
            term = lax.dot_general(left, right, NT, preferred_element_type=F32)
            total = term if total is None else total + term
        return total

    def part_copy(k):
        return remote(part.at[k], part_recv.at[k], sem_part_s.at[k], sem_part_r.at[k], {"tp": 1 - core})

    for k in range(NY):
        for n in range(parts):
            for d in around:
                t_copy(n, k, d).wait_recv()
        part[k] = product(k, 1 - core)
        part_copy(k).start()
        own[k] = product(k, core)
        part_copy(k).wait_recv()
        total = own[k] + part_recv[k]
        for s in range(NX):
            for f in range(2):
                for j in range(width // HD):
                    stage[pl.ds((s * 2 + f) * (width // HD) + j, plane, stride=height), :] = total[
                        (s * 2 + f) * plane : (s * 2 + f + 1) * plane, j * HD : (j + 1) * HD
                    ]
        for i in range(plane // 16):
            block = stage[i * 16 * height : (i + 1) * 16 * height, :]
            o_send[pl.ds(((y + k) % NY) * plane + i * 16, 16)] = block.reshape(16, height, HD).astype(BF16)
        exchange(o_send, o_recv, sem_o, max(k * plane, 1), (k + 1) * plane)
        if k == 0:
            o_recv[me] = o_send[me]

    for n in range(parts):
        exchanged(f_send.at[n], f_recv.at[n], sem_f.at[n]).wait_send()
        for k in range(NY):
            for d in around:
                t_copy(n, k, d).wait_send()
    for k in range(NY):
        part_copy(k).wait_send()
    for e in z_order:
        if e > 0:
            z_copy(e).wait_send()
        for d in around:
            y_copy(e, d).wait_send()

    done = exchanged(o_send, o_recv, sem_o)
    done.wait_recv()
    unpack(o_recv)
    row_at = lax.broadcasted_iota(jnp.int32, (plane, HD), 0)
    low = lax.broadcasted_iota(jnp.int32, (plane, HD), 1) < HD // 2

    def finish(yy, carry):
        for f in range(2):
            alive = row_at + yy * plane < patches[f]

            def piece(xx, j):
                return jnp.concatenate(
                    [stage[pl.ds(((yy * NX + xx) * NZ) * height + (s * 2 + f) * (width // HD) + j, NZ, stride=height), :]
                     for s in range(NX)], axis=0)

            def put(at, value):
                rows = pl.ds(pl.multiple_of(f * PMAX + yy * plane, plane), plane)
                out[rows, at * HD : (at + 1) * HD] = jnp.where(alive, value, F32(0.0)).astype(BF16)

            for m in range(NX // 2):
                left, right = piece(2 * m, 2), piece(2 * m + 1, 2)
                middle = (
                    jnp.where(low, left, right),
                    pltpu.roll(jnp.where(low, right, left), HD // 2, 1),
                )
                for half in range(2):
                    at = half * (NX * third // HD) + m * (2 * third // HD)
                    put(at, piece(2 * m, half))
                    put(at + 1, middle[half])
                    put(at + 2, piece(2 * m + 1, half))
        return carry

    lax.fori_loop(0, NY, finish, 0)
    done.wait_send()


def per_device(q_spatial, k_spatial, v_spatial, q_temporal, k_temporal, out_weight, frame_video, video_patches):
    rows, feats = q_spatial.shape
    heads = feats // HD
    cols = out_weight.shape[1]
    frames = rows // PMAX
    first = lax.axis_index(("grp", "sp")) * frames
    my_video = lax.dynamic_slice_in_dim(frame_video, first, frames)
    match = my_video[:, None] == jnp.arange(video_patches.shape[0], dtype=jnp.int32)[None, :]
    patches = jnp.sum(jnp.where(match, video_patches[None, :], 0), axis=1).astype(jnp.int32)
    by_slot = frame_video.reshape(GROUPS, frames).T.reshape(-1)
    vmem = pl.BlockSpec(memory_space=pltpu.VMEM)
    parts = PARTS
    height = 3 * frames * heads // parts
    all_frames = frame_video.shape[0]
    width = 2 * NZ * cols
    dma = pltpu.SemaphoreType.DMA
    return pl.pallas_call(
        functools.partial(kernel, heads, parts),
        out_shape=jax.ShapeDtypeStruct((rows, feats), BF16),
        in_specs=[vmem] * 8 + [pl.BlockSpec(memory_space=pltpu.SMEM)],
        out_specs=vmem,
        scratch_shapes=[
            pltpu.VMEM((GROUPS * height, HD), F32),
            pltpu.VMEM((parts, GROUPS, height, HD), BF16),
            pltpu.VMEM((parts, GROUPS, height, HD), BF16),
            pltpu.VMEM((GROUPS, height, HD), BF16),
            pltpu.VMEM((GROUPS, height, HD), BF16),
            pltpu.VMEM((parts, NX, NY, all_frames // NY, feats // parts), BF16),
            pltpu.VMEM((NY, NZ, cols, feats), BF16),
            pltpu.VMEM((2 * width, feats), BF16),
            pltpu.VMEM((NY, all_frames, width), F32),
            pltpu.VMEM((NY, all_frames, width), F32),
            pltpu.VMEM((NY, all_frames, width), F32),
            dma((parts, 2)),
            dma((2,)),
            dma((parts, NY, 3)),
            dma((parts, NY, 3)),
            dma((NY,)),
            dma((NY,)),
            dma((NZ,)),
            dma((NZ,)),
            dma((NZ, 3)),
            dma((NZ, 3)),
        ],
        compiler_params=pltpu.CompilerParams(
            collective_id=0, has_side_effects=True, vmem_limit_bytes=58 * 2**20
        ),
    )(
        q_spatial, k_spatial, v_spatial, q_temporal, k_temporal, out_weight,
        by_slot[:, None], by_slot[None, :], patches,
    )


def solution(mesh):
    return jax.shard_map(
        per_device,
        mesh=mesh,
        in_specs=(
            P(("grp", "sp"), "tp"),
            P(("grp", "sp"), "tp"),
            P(("grp", "sp"), "tp"),
            P(("grp", "sp"), "tp"),
            P(("grp", "sp"), "tp"),
            P("tp", ("grp", "sp")),
            P(),
            P(),
        ),
        out_specs=P(("grp", "sp"), "tp"),
        check_vma=False,
    )
```

```python
import functools

import jax
import jax.numpy as jnp
from jax import lax
from jax.experimental import pallas as pl
from jax.experimental.pallas import tpu as pltpu
from jax.sharding import PartitionSpec as P

MESH = pl.DeviceIdType.MESH
HD = 128
PMAX = 128
NY, NX, NZ = 4, 4, 8
GROUPS = NY * NX * NZ
PARTS = 3
LATE = 1
F32 = jnp.float32
BF16 = jnp.bfloat16
NT = (((1,), (1,)), ((), ()))
NN = (((1,), (0,)), ((), ()))


def softmax_rows(masked):
    top = jnp.max(masked, axis=-1, keepdims=True)
    expo = jnp.exp(masked - top)
    return (expo / jnp.sum(expo, axis=-1, keepdims=True)).astype(BF16)


def kernel(
    heads, parts,
    qs_hbm, ks_hbm, vs_hbm, qt_hbm, kt_hbm, w_hbm, videos, frame_video, video_patches,
    out_hbm,
    qs, ks, vs, qt, kt, out, bias, stage, f_send, f_recv, o_send, o_recv, tall, wy, wfull, part, part_recv, own,
    sem_in, sem_out, sem_f, sem_o, sem_t_s, sem_t_r, sem_part_s, sem_part_r, sem_wz_s, sem_wz_r, sem_wy_s, sem_wy_r,
):
    grp = lax.axis_index("grp")
    z = lax.axis_index("sp")
    core = lax.axis_index("tp")
    y, x = grp // NX, grp % NX
    me = grp * NZ + z
    cols = w_hbm.shape[0]
    per = heads // parts
    height = f_send.shape[2]
    plane = NX * NZ

    def load(n, j):
        src, dst = ((qs_hbm, qs), (ks_hbm, ks), (vs_hbm, vs), (qt_hbm, qt), (kt_hbm, kt))[j]
        at = pl.ds(n * per * HD, per * HD)
        return pltpu.make_async_copy(src.at[:, at], dst.at[:, at], sem_in.at[n, j])

    load_w = pltpu.make_async_copy(w_hbm, wy.at[y, z], sem_in.at[parts, 0])
    load_w.start()
    for n in range(parts):
        for j in range(5):
            load(n, j).start()

    def peer(i):
        dy, dx, dz = i // (NX * NZ), (i // NZ) % NX, i % NZ
        g2 = ((y + dy) % NY) * NX + (x + dx) % NX
        return g2, (z + dz) % NZ

    barrier = pltpu.get_barrier_semaphore()

    def greet(i, carry):
        g2, s2 = peer(i)
        pl.semaphore_signal(barrier, inc=1, device_id={"grp": g2, "sp": s2}, device_id_type=MESH)
        return carry

    lax.fori_loop(1, GROUPS, greet, 0)
    pl.semaphore_signal(barrier, inc=1, device_id={"tp": 1 - core}, device_id_type=MESH)

    def remote(src, dst, send, recv, where):
        return pltpu.make_async_remote_copy(
            src_ref=src, dst_ref=dst, send_sem=send, recv_sem=recv, device_id=where, device_id_type=MESH
        )

    patches = [video_patches[frame_video[me * 2 + f]] for f in range(2)]

    frames = videos.shape[1]
    at_row = lax.broadcasted_iota(jnp.int32, (frames, frames), 0)
    at_col = lax.broadcasted_iota(jnp.int32, (frames, frames), 1)
    pick = (at_col == 2 * (at_row % GROUPS) + at_row // GROUPS).astype(F32).astype(BF16)
    wide = jnp.broadcast_to(videos[...], (8, frames)).astype(F32).astype(BF16)
    down = lax.dot_general(pick, wide, NT, preferred_element_type=F32)
    along = lax.dot_general(wide, pick, NT, preferred_element_type=F32)
    bias[...] = jnp.where(down[:, :1] == along[:1, :], F32(0.0), F32(-1e30))

    scale = F32(HD**-0.5)
    key_at = lax.broadcasted_iota(jnp.int32, (PMAX, PMAX), 1)

    def build(n):
        for j in range(5):
            load(n, j).wait()
        for f in range(2):
            rows = slice(f * PMAX, (f + 1) * PMAX)
            for j in range(per):
                at = (rows, slice((n * per + j) * HD, (n * per + j + 1) * HD))
                scores = lax.dot_general(qs[at], ks[at], NT, preferred_element_type=F32) * scale
                probs = softmax_rows(jnp.where(key_at < patches[f], scores, F32(-1e30)))
                value = lax.dot_general(probs, vs[at], NN, preferred_element_type=F32)
                spot = f * per + j
                stage[pl.ds(spot, PMAX, stride=height), :] = qt[at].astype(F32)
                stage[pl.ds(2 * per + spot, PMAX, stride=height), :] = kt[at].astype(F32)
                stage[pl.ds(4 * per + spot, PMAX, stride=height), :] = value

        def pack(i, carry):
            block = stage[pl.ds(pl.multiple_of(i * 16 * height, 16), 16 * height), :]
            f_send[n, pl.ds(i * 16, 16)] = block.reshape(16, height, HD).astype(BF16)
            return carry

        lax.fori_loop(0, GROUPS // 16, pack, 0)

    def unpack(src, yy):
        for i in range(plane // 16):
            block = src[pl.ds(yy * plane + i * 16, 16)].astype(F32)
            at = pl.ds(pl.multiple_of((yy * plane + i * 16) * height, 16), 16 * height)
            stage[at, :] = block.reshape(16 * height, HD)

    def exchange(send_buf, recv_buf, sems, first, last):
        def body(i, carry):
            g2, s2 = peer(i)
            remote(send_buf.at[g2 * NZ + s2], recv_buf.at[me], sems.at[0], sems.at[1], {"grp": g2, "sp": s2}).start()
            return carry

        lax.fori_loop(max(first, 1), last, body, 0)

    def exchanged(send_buf, recv_buf, sems, k):
        some = pl.ds(0, plane if k else plane - 1)
        return remote(send_buf.at[some], recv_buf.at[some], sems.at[0], sems.at[1], {"tp": core})

    def send_part(n, b):
        step = GROUPS // 8
        exchange(f_send.at[n], f_recv.at[n], sem_f.at[n, b * step // plane], b * step, (b + 1) * step)

    def z_copy(step, sign):
        zz = (z - sign * step + NZ) % NZ
        lane = 0 if sign > 0 else 1
        return remote(
            wy.at[y, zz], wy.at[y, zz], sem_wz_s.at[lane, step], sem_wz_r.at[lane, step], {"sp": (z + sign + NZ) % NZ}
        )

    z_plan = ((0, 1), (0, -1), (1, 1), (1, -1), (2, 1), (2, -1), (3, 1))

    def z_next(step):
        for sign in (1, -1):
            if (step, sign) in z_plan:
                z_copy(step, sign).wait_recv()
            if (step + 1, sign) in z_plan:
                z_copy(step + 1, sign).start()

    def y_copy(e, d):
        zz = (z - e + NZ) % NZ
        return remote(
            wy.at[y, zz], wy.at[y, zz], sem_wy_s.at[e, d - 1], sem_wy_r.at[e, d - 1],
            {"grp": ((y + d) % NY) * NX + x},
        )

    def t_copy(n, k, d):
        at = (y + k) % NY
        return remote(
            tall.at[n, x, at], tall.at[n, x, at], sem_t_s.at[n, k, d - 1], sem_t_r.at[n, k, d - 1],
            {"grp": y * NX + (x + d) % NX},
        )

    def t_next(n, k, sign):
        at = (y + k) % NY
        rows = pl.ds(0 if sign > 0 else plane, plane)
        piece = tall.at[n, (x - sign + NX) % NX, at, rows]
        lane = 1 if sign > 0 else 3
        return remote(
            piece, piece, sem_t_s.at[n, k, lane], sem_t_r.at[n, k, lane], {"grp": y * NX + (x + sign + NX) % NX}
        )

    def t_pass(n, k):
        for sign in (1, -1):
            t_copy(n, k, sign % NX).wait_recv()
            t_next(n, k, sign).start()

    def t_rest(n):
        if n < parts - LATE:
            return [functools.partial(t_next, n, sign=s) for s in (1, -1)]
        return [functools.partial(t_copy, n, d=d) for d in around]

    def spread(e):
        for d in around:
            y_copy(e, d).start()

    around = (1, 3, 2)

    build(0)
    load_w.wait()
    pl.semaphore_wait(barrier, GROUPS)
    for sign in (1, -1):
        z_copy(0, sign).start()
    plan = {
        2: (0, (0,)),
        4: (1, (1, 7)),
        6: (2, (2, 6)),
        7: (None, (3, 5)),
    }
    for b in range(8):
        send_part(0, b)
        if b in plan:
            step, shards = plan[b]
            if step is not None:
                z_next(step)
            for e in shards:
                spread(e)
    build(1)
    send_part(1, 0)
    z_next(3)
    spread(4)
    for b in range(1, 8):
        send_part(1, b)
    build(2)
    for n in range(parts):
        f_recv[n, me] = f_send[n, me]

    odd = x % 2
    third = NZ * cols
    small = third // 3

    def order_weights():
        for e in range(NZ):
            for d in around:
                y_copy(e, d).wait_recv()
        for yy in range(NY):
            block = wy[yy].astype(F32).reshape(third, heads * HD)
            base = (yy // 2) * 2 * third
            big = jnp.where(odd == 0, block[: 2 * small], block[small:]).astype(BF16)
            wfull[base + (yy % 2) * 2 * small : base + (yy % 2 + 1) * 2 * small, :] = big
            rest = jnp.where(odd == 0, block[2 * small :], block[:small]).astype(BF16)
            spot = odd + (yy % 2) - 2 * odd * (yy % 2)
            wfull[pl.ds(pl.multiple_of(base + 4 * small + spot * small, 16), small), :] = rest

    for n in range(parts):
        if 0 < n <= parts - LATE:
            for k in range(NY):
                t_pass(n - 1, k)
        for k in range(NY):
            exchanged(f_send.at[n], f_recv.at[n], sem_f.at[n, k], k).wait_recv()
            unpack(f_recv.at[n], (y - k + NY) % NY)
        for j in range(per):
            q, k, v = (
                jnp.concatenate(
                    [stage[pl.ds(t * 2 * per + f * per + j, GROUPS, stride=height), :] for f in range(2)], axis=0
                ).astype(BF16)
                for t in range(3)
            )
            scores = lax.dot_general(q, k, NT, preferred_element_type=F32) * scale
            probs = softmax_rows(scores + bias[...])
            value = lax.dot_general(probs, v, NN, preferred_element_type=F32)
            for k in range(NY):
                for f in range(2):
                    rows = value[f * GROUPS + k * plane : f * GROUPS + (k + 1) * plane]
                    tall[n, x, k, f * plane : (f + 1) * plane, j * HD : (j + 1) * HD] = rows.astype(BF16)
        for k in range(NY):
            if n < parts - 1:
                send_part(parts - 1, n * NY + k)
            for d in (1, 3) if n < parts - LATE else around:
                t_copy(n, k, d).start()

    order_weights()

    width = 2 * third
    feats = per * HD

    def product(k, c, groups):
        total = None
        for n in groups:
            left = jnp.concatenate([tall[n, s, (y + k) % NY] for s in range(NX)], axis=0)
            right = wfull[pl.ds(pl.multiple_of(c * width, 16), width), n * feats : (n + 1) * feats]
            term = lax.dot_general(left, right, NT, preferred_element_type=F32)
            total = term if total is None else total + term
        return total

    def part_copy(k):
        return remote(part.at[k], part_recv.at[k], sem_part_s.at[k], sem_part_r.at[k], {"tp": 1 - core})

    for k in range(NY):
        for n in range(parts - 1):
            for c in t_rest(n):
                c(k=k).wait_recv()
        part[k] = product(k, 1 - core, range(parts - 1))
        own[k] = product(k, core, range(parts - 1))

    for k in range(NY):
        if not LATE:
            for i in ((0, 1), (2,), (3,), ())[k]:
                t_pass(parts - 1, i)
        for c in t_rest(parts - 1):
            c(k=k).wait_recv()
        part[k] += product(k, 1 - core, (parts - 1,))
        part_copy(k).start()
        own[k] += product(k, core, (parts - 1,))
        part_copy(k).wait_recv()
        total = own[k] + part_recv[k]
        for s in range(NX):
            for f in range(2):
                for j in range(width // HD):
                    stage[pl.ds((s * 2 + f) * (width // HD) + j, plane, stride=height), :] = total[
                        (s * 2 + f) * plane : (s * 2 + f + 1) * plane, j * HD : (j + 1) * HD
                    ]
        for i in range(plane // 16):
            block = stage[i * 16 * height : (i + 1) * 16 * height, :]
            o_send[pl.ds(((y + k) % NY) * plane + i * 16, 16)] = block.reshape(16, height, HD).astype(BF16)
        exchange(o_send, o_recv, sem_o.at[k], k * plane, (k + 1) * plane)
        if k == 0:
            o_recv[me] = o_send[me]

    for n in range(parts):
        for k in range(NY):
            exchanged(f_send.at[n], f_recv.at[n], sem_f.at[n, k], k).wait_send()
            for d in (1, 3) if n < parts - LATE else around:
                t_copy(n, k, d).wait_send()
            if n < parts - LATE:
                for sign in (1, -1):
                    t_next(n, k, sign).wait_send()
    for k in range(NY):
        part_copy(k).wait_send()
    for step, sign in z_plan:
        z_copy(step, sign).wait_send()
    for e in range(NZ):
        for d in around:
            y_copy(e, d).wait_send()

    row_at = lax.broadcasted_iota(jnp.int32, (plane, HD), 0)
    low = lax.broadcasted_iota(jnp.int32, (plane, HD), 1) < HD // 2

    def store(yy, f, k):
        rows = pl.ds(pl.multiple_of(f * PMAX + yy * plane, plane), plane)
        return pltpu.make_async_copy(out.at[rows], out_hbm.at[rows], sem_out.at[k, f])

    def finish(yy):
        for f in range(2):
            alive = row_at + yy * plane < patches[f]

            def piece(xx, j):
                return jnp.concatenate(
                    [stage[pl.ds(((yy * NX + xx) * NZ) * height + (s * 2 + f) * (width // HD) + j, NZ, stride=height), :]
                     for s in range(NX)], axis=0)

            def put(at, value):
                rows = pl.ds(pl.multiple_of(f * PMAX + yy * plane, plane), plane)
                out[rows, at * HD : (at + 1) * HD] = jnp.where(alive, value, F32(0.0)).astype(BF16)

            for m in range(NX // 2):
                left, right = piece(2 * m, 2), piece(2 * m + 1, 2)
                middle = (
                    jnp.where(low, left, right),
                    pltpu.roll(jnp.where(low, right, left), HD // 2, 1),
                )
                for half in range(2):
                    at = half * (NX * third // HD) + m * (2 * third // HD)
                    put(at, piece(2 * m, half))
                    put(at + 1, middle[half])
                    put(at + 2, piece(2 * m + 1, half))

    for k in range(NY):
        yy = (y - k + NY) % NY
        exchanged(o_send, o_recv, sem_o.at[k], k).wait_recv()
        unpack(o_recv, yy)
        finish(yy)
        for f in range(2):
            store(yy, f, k).start()
    for k in range(NY):
        exchanged(o_send, o_recv, sem_o.at[k], k).wait_send()
        for f in range(2):
            store((y - k + NY) % NY, f, k).wait()


def per_device(q_spatial, k_spatial, v_spatial, q_temporal, k_temporal, out_weight, frame_video, video_patches):
    rows, feats = q_spatial.shape
    heads = feats // HD
    cols = out_weight.shape[1]
    frames = rows // PMAX
    anywhere = pl.BlockSpec(memory_space=pl.ANY)
    scalars = pl.BlockSpec(memory_space=pltpu.SMEM)
    parts = PARTS
    height = 3 * frames * heads // parts
    all_frames = frame_video.shape[0]
    width = 2 * NZ * cols
    dma = pltpu.SemaphoreType.DMA
    return pl.pallas_call(
        functools.partial(kernel, heads, parts),
        out_shape=jax.ShapeDtypeStruct((rows, feats), BF16),
        in_specs=[anywhere] * 6 + [pl.BlockSpec(memory_space=pltpu.VMEM), scalars, scalars],
        out_specs=anywhere,
        scratch_shapes=[pltpu.VMEM((rows, feats), BF16)] * 6 + [
            pltpu.VMEM((all_frames, all_frames), F32),
            pltpu.VMEM((GROUPS * height, HD), F32),
            pltpu.VMEM((parts, GROUPS, height, HD), BF16),
            pltpu.VMEM((parts, GROUPS, height, HD), BF16),
            pltpu.VMEM((GROUPS, height, HD), BF16),
            pltpu.VMEM((GROUPS, height, HD), BF16),
            pltpu.VMEM((parts, NX, NY, all_frames // NY, feats // parts), BF16),
            pltpu.VMEM((NY, NZ, cols, feats), BF16),
            pltpu.VMEM((2 * width, feats), BF16),
            pltpu.VMEM((NY, all_frames, width), F32),
            pltpu.VMEM((NY, all_frames, width), F32),
            pltpu.VMEM((NY, all_frames, width), F32),
            dma((parts + 1, 5)),
            dma((NY, 2)),
            dma((parts, NY, 2)),
            dma((NY, 2)),
            dma((parts, NY, 4)),
            dma((parts, NY, 4)),
            dma((NY,)),
            dma((NY,)),
            dma((2, 4)),
            dma((2, 4)),
            dma((NZ, 3)),
            dma((NZ, 3)),
        ],
        compiler_params=pltpu.CompilerParams(
            collective_id=0, has_side_effects=True, vmem_limit_bytes=58 * 2**20
        ),
    )(
        q_spatial, k_spatial, v_spatial, q_temporal, k_temporal, out_weight.T,
        frame_video[None, :], frame_video, video_patches,
    )


def solution(mesh):
    return jax.shard_map(
        per_device,
        mesh=mesh,
        in_specs=(
            P(("grp", "sp"), "tp"),
            P(("grp", "sp"), "tp"),
            P(("grp", "sp"), "tp"),
            P(("grp", "sp"), "tp"),
            P(("grp", "sp"), "tp"),
            P("tp", ("grp", "sp")),
            P(),
            P(),
        ),
        out_specs=P(("grp", "sp"), "tp"),
        check_vma=False,
    )
```

```python
import functools

import jax
import jax.numpy as jnp
from jax import lax
from jax.experimental import pallas as pl
from jax.experimental.pallas import tpu as pltpu
from jax.sharding import PartitionSpec as P

MESH = pl.DeviceIdType.MESH
HD = 128
PMAX = 128
NY, NX, NZ = 4, 4, 8
GROUPS = NY * NX * NZ
PARTS = 3
LATE = 1
F32 = jnp.float32
BF16 = jnp.bfloat16
NT = (((1,), (1,)), ((), ()))
NN = (((1,), (0,)), ((), ()))


def softmax_rows(masked):
    top = jnp.max(masked, axis=-1, keepdims=True)
    expo = jnp.exp(masked - top)
    return (expo / jnp.sum(expo, axis=-1, keepdims=True)).astype(BF16)


def kernel(
    heads, parts,
    qs_hbm, ks_hbm, vs_hbm, qt_hbm, kt_hbm, w_hbm, videos, frame_video, video_patches,
    out_hbm,
    qs, ks, vs, qt, kt, out, bias, stage, f_send, f_recv, o_send, o_recv, tall, wy, wfull, part, part_recv, own,
    sem_in, sem_out, sem_f, sem_o, sem_t_s, sem_t_r, sem_part_s, sem_part_r, sem_wz_s, sem_wz_r, sem_wy_s, sem_wy_r,
):
    grp = lax.axis_index("grp")
    z = lax.axis_index("sp")
    core = lax.axis_index("tp")
    y, x = grp // NX, grp % NX
    me = grp * NZ + z
    cols = w_hbm.shape[0]
    per = heads // parts
    height = f_send.shape[2]
    plane = NX * NZ

    def load(n, j):
        src, dst = ((qs_hbm, qs), (ks_hbm, ks), (vs_hbm, vs), (qt_hbm, qt), (kt_hbm, kt))[j]
        at = pl.ds(n * per * HD, per * HD)
        return pltpu.make_async_copy(src.at[:, at], dst.at[:, at], sem_in.at[n, j])

    load_w = pltpu.make_async_copy(w_hbm, wy.at[y, z], sem_in.at[parts, 0])
    load_w.start()
    for n in range(parts):
        for j in range(5):
            load(n, j).start()

    def peer(i):
        dy, dx, dz = i // (NX * NZ), (i // NZ) % NX, i % NZ
        g2 = ((y + dy) % NY) * NX + (x + dx) % NX
        return g2, (z + dz) % NZ

    barrier = pltpu.get_barrier_semaphore()

    def greet(i, carry):
        g2, s2 = peer(i)
        pl.semaphore_signal(barrier, inc=1, device_id={"grp": g2, "sp": s2}, device_id_type=MESH)
        return carry

    lax.fori_loop(1, GROUPS, greet, 0)
    pl.semaphore_signal(barrier, inc=1, device_id={"tp": 1 - core}, device_id_type=MESH)

    def remote(src, dst, send, recv, where):
        return pltpu.make_async_remote_copy(
            src_ref=src, dst_ref=dst, send_sem=send, recv_sem=recv, device_id=where, device_id_type=MESH
        )

    patches = [video_patches[frame_video[me * 2 + f]] for f in range(2)]

    frames = videos.shape[1]
    at_row = lax.broadcasted_iota(jnp.int32, (frames, frames), 0)
    at_col = lax.broadcasted_iota(jnp.int32, (frames, frames), 1)
    pick = (at_col == 2 * (at_row % GROUPS) + at_row // GROUPS).astype(F32).astype(BF16)
    wide = jnp.broadcast_to(videos[...], (8, frames)).astype(F32).astype(BF16)
    down = lax.dot_general(pick, wide, NT, preferred_element_type=F32)
    along = lax.dot_general(wide, pick, NT, preferred_element_type=F32)
    bias[...] = jnp.where(down[:, :1] == along[:1, :], F32(0.0), F32(-1e30))

    scale = F32(HD**-0.5)
    key_at = lax.broadcasted_iota(jnp.int32, (PMAX, PMAX), 1)

    def build(n):
        for j in range(5):
            load(n, j).wait()
        for f in range(2):
            rows = slice(f * PMAX, (f + 1) * PMAX)
            for j in range(per):
                at = (rows, slice((n * per + j) * HD, (n * per + j + 1) * HD))
                scores = lax.dot_general(qs[at], ks[at], NT, preferred_element_type=F32) * scale
                probs = softmax_rows(jnp.where(key_at < patches[f], scores, F32(-1e30)))
                value = lax.dot_general(probs, vs[at], NN, preferred_element_type=F32)
                spot = f * per + j
                stage[pl.ds(spot, PMAX, stride=height), :] = qt[at].astype(F32)
                stage[pl.ds(2 * per + spot, PMAX, stride=height), :] = kt[at].astype(F32)
                stage[pl.ds(4 * per + spot, PMAX, stride=height), :] = value

        def pack(i, carry):
            block = stage[pl.ds(pl.multiple_of(i * 16 * height, 16), 16 * height), :]
            f_send[n, pl.ds(i * 16, 16)] = block.reshape(16, height, HD).astype(BF16)
            return carry

        lax.fori_loop(0, GROUPS // 16, pack, 0)

    def unpack(src, yy):
        for i in range(plane // 16):
            block = src[pl.ds(yy * plane + i * 16, 16)].astype(F32)
            at = pl.ds(pl.multiple_of((yy * plane + i * 16) * height, 16), 16 * height)
            stage[at, :] = block.reshape(16 * height, HD)

    def exchange(send_buf, recv_buf, sems, first, last):
        def body(j, carry):
            g2, s2 = peer(first + ((j - first) * 13) % plane)
            remote(send_buf.at[g2 * NZ + s2], recv_buf.at[me], sems.at[0], sems.at[1], {"grp": g2, "sp": s2}).start()
            return carry

        lax.fori_loop(max(first, 1), last, body, 0)

    def exchanged(send_buf, recv_buf, sems, k):
        some = pl.ds(0, plane if k else plane - 1)
        return remote(send_buf.at[some], recv_buf.at[some], sems.at[0], sems.at[1], {"tp": core})

    def send_part(n, b):
        step = GROUPS // 8

        def body(j, carry):
            i = (j * 37) % GROUPS
            g2, s2 = peer(i)
            remote(
                f_send.at[n, g2 * NZ + s2], f_recv.at[n, me], sem_f.at[n, i // plane, 0], sem_f.at[n, i // plane, 1],
                {"grp": g2, "sp": s2},
            ).start()
            return carry

        lax.fori_loop(max(b * step, 1), (b + 1) * step, body, 0)

    def z_copy(step, sign):
        zz = (z - sign * step + NZ) % NZ
        lane = 0 if sign > 0 else 1
        return remote(
            wy.at[y, zz], wy.at[y, zz], sem_wz_s.at[lane, step], sem_wz_r.at[lane, step], {"sp": (z + sign + NZ) % NZ}
        )

    z_plan = ((0, 1), (0, -1), (1, 1), (1, -1), (2, 1), (2, -1), (3, 1))

    def z_next(step):
        for sign in (1, -1):
            if (step, sign) in z_plan:
                z_copy(step, sign).wait_recv()
            if (step + 1, sign) in z_plan:
                z_copy(step + 1, sign).start()

    def y_copy(e, d):
        zz = (z - e + NZ) % NZ
        return remote(
            wy.at[y, zz], wy.at[y, zz], sem_wy_s.at[e, d - 1], sem_wy_r.at[e, d - 1],
            {"grp": ((y + d) % NY) * NX + x},
        )

    def t_copy(n, k, d):
        at = (y + k) % NY
        return remote(
            tall.at[n, x, at], tall.at[n, x, at], sem_t_s.at[n, k, d - 1], sem_t_r.at[n, k, d - 1],
            {"grp": y * NX + (x + d) % NX},
        )

    def t_next(n, k, sign):
        at = (y + k) % NY
        rows = pl.ds(0 if sign > 0 else plane, plane)
        piece = tall.at[n, (x - sign + NX) % NX, at, rows]
        lane = 1 if sign > 0 else 3
        return remote(
            piece, piece, sem_t_s.at[n, k, lane], sem_t_r.at[n, k, lane], {"grp": y * NX + (x + sign + NX) % NX}
        )

    def t_pass(n, k):
        for sign in (1, -1):
            t_copy(n, k, sign % NX).wait_recv()
            t_next(n, k, sign).start()

    def t_rest(n):
        if n < parts - LATE:
            return [functools.partial(t_next, n, sign=s) for s in (1, -1)]
        return [functools.partial(t_copy, n, d=d) for d in around]

    def spread(e):
        for d in around:
            y_copy(e, d).start()

    around = (1, 3, 2)

    build(0)
    load_w.wait()
    pl.semaphore_wait(barrier, GROUPS)
    for sign in (1, -1):
        z_copy(0, sign).start()
    plan = {
        2: (0, (0,)),
        4: (1, (1, 7)),
        6: (2, (2, 6)),
        7: (None, (3, 5)),
    }
    for b in range(8):
        send_part(0, b)
        if b in plan:
            step, shards = plan[b]
            if step is not None:
                z_next(step)
            for e in shards:
                spread(e)
    build(1)
    send_part(1, 0)
    z_next(3)
    spread(4)
    for b in range(1, 8):
        send_part(1, b)
    build(2)
    for n in range(parts):
        f_recv[n, me] = f_send[n, me]

    odd = x % 2
    third = NZ * cols
    small = third // 3

    def order_weights():
        for e in range(NZ):
            for d in around:
                y_copy(e, d).wait_recv()
        for yy in range(NY):
            block = wy[yy].astype(F32).reshape(third, heads * HD)
            base = (yy // 2) * 2 * third
            big = jnp.where(odd == 0, block[: 2 * small], block[small:]).astype(BF16)
            wfull[base + (yy % 2) * 2 * small : base + (yy % 2 + 1) * 2 * small, :] = big
            rest = jnp.where(odd == 0, block[2 * small :], block[:small]).astype(BF16)
            spot = odd + (yy % 2) - 2 * odd * (yy % 2)
            wfull[pl.ds(pl.multiple_of(base + 4 * small + spot * small, 16), small), :] = rest

    for n in range(parts):
        if 0 < n <= parts - LATE:
            for k in range(NY):
                t_pass(n - 1, k)
        for k in range(NY):
            exchanged(f_send.at[n], f_recv.at[n], sem_f.at[n, k], k).wait_recv()
            unpack(f_recv.at[n], (y - k + NY) % NY)
        for j in range(per):
            q, k, v = (
                jnp.concatenate(
                    [stage[pl.ds(t * 2 * per + f * per + j, GROUPS, stride=height), :] for f in range(2)], axis=0
                ).astype(BF16)
                for t in range(3)
            )
            scores = lax.dot_general(q, k, NT, preferred_element_type=F32) * scale
            probs = softmax_rows(scores + bias[...])
            value = lax.dot_general(probs, v, NN, preferred_element_type=F32)
            for k in range(NY):
                for f in range(2):
                    rows = value[f * GROUPS + k * plane : f * GROUPS + (k + 1) * plane]
                    tall[n, x, k, f * plane : (f + 1) * plane, j * HD : (j + 1) * HD] = rows.astype(BF16)
        for k in range(NY):
            if n < parts - 1:
                send_part(parts - 1, n * NY + k)
            for d in (1, 3) if n < parts - LATE else around:
                t_copy(n, k, d).start()

    order_weights()

    width = 2 * third
    feats = per * HD

    def product(k, c, groups):
        total = None
        for n in groups:
            left = jnp.concatenate([tall[n, s, (y + k) % NY] for s in range(NX)], axis=0)
            right = wfull[pl.ds(pl.multiple_of(c * width, 16), width), n * feats : (n + 1) * feats]
            term = lax.dot_general(left, right, NT, preferred_element_type=F32)
            total = term if total is None else total + term
        return total

    def part_copy(k):
        return remote(part.at[k], part_recv.at[k], sem_part_s.at[k], sem_part_r.at[k], {"tp": 1 - core})

    for k in range(NY):
        for n in range(parts - 1):
            for c in t_rest(n):
                c(k=k).wait_recv()
        part[k] = product(k, 1 - core, range(parts - 1))
        own[k] = product(k, core, range(parts - 1))

    for k in range(NY):
        if not LATE:
            for i in ((0, 1), (2,), (3,), ())[k]:
                t_pass(parts - 1, i)
        for c in t_rest(parts - 1):
            c(k=k).wait_recv()
        part[k] += product(k, 1 - core, (parts - 1,))
        part_copy(k).start()
        own[k] += product(k, core, (parts - 1,))
        part_copy(k).wait_recv()
        total = own[k] + part_recv[k]
        for s in range(NX):
            for f in range(2):
                for j in range(width // HD):
                    stage[pl.ds((s * 2 + f) * (width // HD) + j, plane, stride=height), :] = total[
                        (s * 2 + f) * plane : (s * 2 + f + 1) * plane, j * HD : (j + 1) * HD
                    ]
        for i in range(plane // 16):
            block = stage[i * 16 * height : (i + 1) * 16 * height, :]
            o_send[pl.ds(((y + k) % NY) * plane + i * 16, 16)] = block.reshape(16, height, HD).astype(BF16)
        exchange(o_send, o_recv, sem_o.at[k], k * plane, (k + 1) * plane)
        if k == 0:
            o_recv[me] = o_send[me]

    for n in range(parts):
        for k in range(NY):
            exchanged(f_send.at[n], f_recv.at[n], sem_f.at[n, k], k).wait_send()
            for d in (1, 3) if n < parts - LATE else around:
                t_copy(n, k, d).wait_send()
            if n < parts - LATE:
                for sign in (1, -1):
                    t_next(n, k, sign).wait_send()
    for k in range(NY):
        part_copy(k).wait_send()
    for step, sign in z_plan:
        z_copy(step, sign).wait_send()
    for e in range(NZ):
        for d in around:
            y_copy(e, d).wait_send()

    row_at = lax.broadcasted_iota(jnp.int32, (plane, HD), 0)
    low = lax.broadcasted_iota(jnp.int32, (plane, HD), 1) < HD // 2

    def store(yy, f, k):
        rows = pl.ds(pl.multiple_of(f * PMAX + yy * plane, plane), plane)
        return pltpu.make_async_copy(out.at[rows], out_hbm.at[rows], sem_out.at[k, f])

    def finish(yy):
        for f in range(2):
            alive = row_at + yy * plane < patches[f]

            def piece(xx, j):
                return jnp.concatenate(
                    [stage[pl.ds(((yy * NX + xx) * NZ) * height + (s * 2 + f) * (width // HD) + j, NZ, stride=height), :]
                     for s in range(NX)], axis=0)

            def put(at, value):
                rows = pl.ds(pl.multiple_of(f * PMAX + yy * plane, plane), plane)
                out[rows, at * HD : (at + 1) * HD] = jnp.where(alive, value, F32(0.0)).astype(BF16)

            for m in range(NX // 2):
                left, right = piece(2 * m, 2), piece(2 * m + 1, 2)
                middle = (
                    jnp.where(low, left, right),
                    pltpu.roll(jnp.where(low, right, left), HD // 2, 1),
                )
                for half in range(2):
                    at = half * (NX * third // HD) + m * (2 * third // HD)
                    put(at, piece(2 * m, half))
                    put(at + 1, middle[half])
                    put(at + 2, piece(2 * m + 1, half))

    for k in range(NY):
        yy = (y - k + NY) % NY
        exchanged(o_send, o_recv, sem_o.at[k], k).wait_recv()
        unpack(o_recv, yy)
        finish(yy)
        for f in range(2):
            store(yy, f, k).start()
    for k in range(NY):
        exchanged(o_send, o_recv, sem_o.at[k], k).wait_send()
        for f in range(2):
            store((y - k + NY) % NY, f, k).wait()


def per_device(q_spatial, k_spatial, v_spatial, q_temporal, k_temporal, out_weight, frame_video, video_patches):
    rows, feats = q_spatial.shape
    heads = feats // HD
    cols = out_weight.shape[1]
    frames = rows // PMAX
    anywhere = pl.BlockSpec(memory_space=pl.ANY)
    scalars = pl.BlockSpec(memory_space=pltpu.SMEM)
    parts = PARTS
    height = 3 * frames * heads // parts
    all_frames = frame_video.shape[0]
    width = 2 * NZ * cols
    dma = pltpu.SemaphoreType.DMA
    return pl.pallas_call(
        functools.partial(kernel, heads, parts),
        out_shape=jax.ShapeDtypeStruct((rows, feats), BF16),
        in_specs=[anywhere] * 6 + [pl.BlockSpec(memory_space=pltpu.VMEM), scalars, scalars],
        out_specs=anywhere,
        scratch_shapes=[pltpu.VMEM((rows, feats), BF16)] * 6 + [
            pltpu.VMEM((all_frames, all_frames), F32),
            pltpu.VMEM((GROUPS * height, HD), F32),
            pltpu.VMEM((parts, GROUPS, height, HD), BF16),
            pltpu.VMEM((parts, GROUPS, height, HD), BF16),
            pltpu.VMEM((GROUPS, height, HD), BF16),
            pltpu.VMEM((GROUPS, height, HD), BF16),
            pltpu.VMEM((parts, NX, NY, all_frames // NY, feats // parts), BF16),
            pltpu.VMEM((NY, NZ, cols, feats), BF16),
            pltpu.VMEM((2 * width, feats), BF16),
            pltpu.VMEM((NY, all_frames, width), F32),
            pltpu.VMEM((NY, all_frames, width), F32),
            pltpu.VMEM((NY, all_frames, width), F32),
            dma((parts + 1, 5)),
            dma((NY, 2)),
            dma((parts, NY, 2)),
            dma((NY, 2)),
            dma((parts, NY, 4)),
            dma((parts, NY, 4)),
            dma((NY,)),
            dma((NY,)),
            dma((2, 4)),
            dma((2, 4)),
            dma((NZ, 3)),
            dma((NZ, 3)),
        ],
        compiler_params=pltpu.CompilerParams(
            collective_id=0, has_side_effects=True, vmem_limit_bytes=58 * 2**20
        ),
    )(
        q_spatial, k_spatial, v_spatial, q_temporal, k_temporal, out_weight.T,
        frame_video[None, :], frame_video, video_patches,
    )


def solution(mesh):
    return jax.shard_map(
        per_device,
        mesh=mesh,
        in_specs=(
            P(("grp", "sp"), "tp"),
            P(("grp", "sp"), "tp"),
            P(("grp", "sp"), "tp"),
            P(("grp", "sp"), "tp"),
            P(("grp", "sp"), "tp"),
            P("tp", ("grp", "sp")),
            P(),
            P(),
        ),
        out_specs=P(("grp", "sp"), "tp"),
        check_vma=False,
    )
```
